512 devices in a mesh: ctx: 256 (over z, y_lo, x, core), mp: 2 (over y_hi).
Axes of the slice: x: 4, y: 4 (y_hi: 2, y_lo: 2; y = y_hi * 2 + y_lo), z: 16, core: 2. Of those that a mesh axis runs over, the one named last changes fastest.
Arguments:
- queries: bfloat16 [32768, 1024], P('ctx', 'mp'), may hold values from -6 to 6
- keys: bfloat16 [32768, 1024], P('ctx', 'mp'), may hold values from -6 to 6
- values: bfloat16 [3, 32768, 1024], P(None, 'ctx', 'mp'), may hold values from -6 to 6
- tile_mask: int32 [256, 15, 1, 1], P('ctx'), may hold values 0 or 1
Outputs:
- attended: bfloat16 [3, 32768, 1024], P(None, 'ctx', 'mp')
The draws below stay inside these ranges and needn't reach their ends.
All inputs are finite; a program needn't handle non-finite values. No bound on the sum of `tile_mask` on one device may be relied on, other than what follows from the above.
Results may differ from the reference program's by a relative error of at most 0.0049.
Values may be sent and summed in bfloat16 or wider, within the bound.
No kernel may reach another device: no remote copies, remote signals or barrier semaphores. Data moves between devices by JAX's collectives and lax.ppermute only.
A program may use at most 64 MiB of HBM per device.

```python
import math
import jax
import jax.numpy as jnp
from jax import lax

BLK = 128
TILE = 128
HEADS = 8
HD = 128
LAYERS = 3
NBLK = 256
LEVELS = 7
OFFS = 15
TILES = 1
TOKENS = 32768
HQ = 1024


def draw_queries(key, part):
    key = jax.random.fold_in(key, 7)
    result = jnp.clip(jax.random.normal(key, (TOKENS, HEADS * HD), jnp.float32), -6.0, 6.0)
    return result.astype(jnp.bfloat16)


def draw_keys(key, part):
    key = jax.random.fold_in(key, 13)
    result = jnp.clip(jax.random.normal(key, (TOKENS, HEADS * HD), jnp.float32), -6.0, 6.0)
    return result.astype(jnp.bfloat16)


def place_ends(values, rng, smallest, high):
    spot = [jax.random.randint(jax.random.fold_in(rng, axis), (), 0, length) for axis, length in enumerate(values.shape)]
    main_axis = values.shape.index(max(values.shape))
    next_to = spot[:main_axis] + [(spot[main_axis] + 1) % values.shape[main_axis]] + spot[main_axis + 1:]
    return values.at[tuple(spot)].set(smallest).at[tuple(next_to)].set(high)


def shard_levels(rng, shape, pieces, low, high):
    def one(dim, parts):
        steps = jax.random.uniform(jax.random.fold_in(jax.random.fold_in(rng, 6), dim), (parts,), jnp.float32, low / len(pieces), high / len(pieces))
        return jnp.repeat(jnp.exp(steps), shape[dim] // parts).reshape((-1,) + (1,) * (len(shape) - dim - 1))

    level = one(*pieces[0])
    for cut in pieces[1:]:
        level = level * one(*cut)
    return level


def normal_values(rng, shape, width, limit, shards=(), kind=jnp.bfloat16):
    factor_of = shard_levels(rng, shape, shards, -0.22, 0.18) if shards else 1.0
    values = jax.random.normal(rng, shape, jnp.float32) * width * factor_of
    return jnp.minimum(jnp.maximum(values, -limit), limit).astype(kind)


def setup_inputs(seed: int = 0) -> dict:
    arg_keys = jax.random.split(jax.random.key(seed), 5)
    return {
        "queries": draw_queries(jax.random.fold_in(arg_keys[4], 71), 0),
        "keys": draw_keys(jax.random.fold_in(arg_keys[4], 71), 0),
        "values": normal_values(arg_keys[2], (LAYERS, TOKENS, HQ), 1.0, 6.0, ((1, 256), (2, 2))),
        "tile_mask": place_ends((jax.random.randint(arg_keys[3], (NBLK, OFFS, TILES, TILES), 0, 2) < 1).astype(jnp.int32), jax.random.fold_in(arg_keys[3], 1), 0, 1),
    }


def expand_live(mask_block):
    offset_ids = lax.broadcasted_iota(jnp.int32, mask_block.shape, 0)
    query_tiles = lax.broadcasted_iota(jnp.int32, mask_block.shape, 1)
    key_tiles = lax.broadcasted_iota(jnp.int32, mask_block.shape, 2)
    live = (mask_block != 0) | (offset_ids == 0) & (query_tiles == key_tiles)
    return jnp.transpose(live, (1, 0, 2))[:, None, :, :, None]

def block_attention(query_block, key_stack, value_stack, mask_block):
    scale = 1.0 / math.sqrt(HD)
    query_heads = query_block.astype(jnp.float32).reshape(BLK, HEADS, HD)
    key_heads = key_stack.astype(jnp.float32).reshape(OFFS, BLK, HEADS, HD)
    scores = jnp.einsum('qhd,okhd->hqok', query_heads, key_heads) * scale
    shaped = scores.reshape(HEADS, TILES, TILE, OFFS, TILES, TILE)
    live = expand_live(mask_block)[None]
    masked = jnp.where(live, shaped, -1e+30)
    largest = lax.optimization_barrier(jnp.max(masked, axis=(3, 4, 5), keepdims=True))
    expval = jnp.where(live, jnp.exp(masked - largest), 0.0)
    totals = lax.optimization_barrier(jnp.sum(expval, axis=(3, 4, 5), keepdims=True))
    weights = (expval / totals).astype(jnp.bfloat16).reshape(HEADS, BLK, OFFS, BLK)
    value_heads = value_stack.astype(jnp.float32).reshape(LAYERS, OFFS, BLK, HEADS, HD)
    result = jnp.einsum('hqok,lokhd->lqhd', weights.astype(jnp.float32), value_heads)
    return result.reshape(LAYERS, BLK, HQ).astype(jnp.bfloat16)

def reference(queries, keys, values, tile_mask):
    offset_list = [0]
    for degree in range(LEVELS):
        offset_list.append(2 ** degree)
        offset_list.append(-2 ** degree)
    offsets = jnp.array(offset_list, dtype=jnp.int32)
    query_blocks = queries.reshape(NBLK, BLK, HQ)
    key_blocks = keys.reshape(NBLK, BLK, HQ)
    value_blocks = values.reshape(LAYERS, NBLK, BLK, HQ)

    def one_block(index):
        targets = ((index + offsets) % NBLK).astype(jnp.int32)
        key_stack = key_blocks[targets]
        value_stack = value_blocks[:, targets]
        return block_attention(query_blocks[index], key_stack, value_stack, tile_mask[index])
    results = lax.map(one_block, jnp.arange(NBLK, dtype=jnp.int32))
    return jnp.transpose(results, (1, 0, 2, 3)).reshape(LAYERS, TOKENS, HQ)
```

```python
import functools
import math

import jax
import jax.numpy as jnp
from jax import lax
from jax.experimental import pallas as pl
from jax.experimental.pallas import tpu as pltpu
from jax.sharding import PartitionSpec as P

HD = 128
DEAD = -1e30
ZS, YS, XS, CS = 16, 2, 4, 2


def place(z, y, x, c):
    return (((z % ZS) * YS + y % YS) * XS + x % XS) * CS + c % CS


def send(block, target):
    pairs = []
    for z in range(ZS):
        for y in range(YS):
            for x in range(XS):
                for c in range(CS):
                    goal = target(z, y, x, c)
                    if goal is not None:
                        pairs.append((place(z, y, x, c), place(*goal)))
    return lax.ppermute(block, "ctx", pairs)


def part_kernel(count, first, last, q_ref, live_ref, *refs):
    blocks = refs[:count]
    rest = refs[count:]
    if not first:
        acc_in, max_in, sum_in = rest[:3]
        rest = rest[3:]
    if last:
        (out_ref,) = rest
    else:
        acc_out, max_out, sum_out = rest
    layers = blocks[0].shape[0] - 1
    rows = q_ref.shape[0]
    factor = math.log2(math.e) / math.sqrt(HD)
    for head in range(q_ref.shape[1] // HD):
        window = slice(head * HD, (head + 1) * HD)
        q = q_ref[:, window]
        scores = []
        for j in range(count):
            s = lax.dot_general(
                q, blocks[j][0, :, window], (((1,), (1,)), ((), ())),
                preferred_element_type=jnp.float32,
            ) * factor
            scores.append(jnp.where(live_ref[j] != 0, s, DEAD))
        top = functools.reduce(jnp.maximum, scores)
        largest = jnp.max(top, axis=1, keepdims=True)
        if not first:
            before = max_in[head, :, :1]
            largest = jnp.maximum(largest, before)
            shrink = jnp.exp2(before - largest)
        probs = [jnp.exp2(s - largest) for s in scores]
        total = jnp.sum(functools.reduce(jnp.add, probs), axis=1, keepdims=True)
        if not first:
            total = total + sum_in[head, :, :1] * shrink
        probs = [p.astype(jnp.bfloat16) for p in probs]
        for layer in range(layers):
            acc = functools.reduce(jnp.add, [
                jnp.dot(probs[j], blocks[j][1 + layer, :, window], preferred_element_type=jnp.float32)
                for j in range(count)
            ])
            if not first:
                acc = acc + acc_in[layer, :, window] * shrink
            if last:
                out_ref[layer, :, window] = (acc / total).astype(out_ref.dtype)
            else:
                acc_out[layer, :, window] = acc
        if not last:
            max_out[head] = jnp.broadcast_to(largest, (rows, HD))
            sum_out[head] = jnp.broadcast_to(total, (rows, HD))


def attend(queries, blocks, live, state=None, last=False):
    rows, width = queries.shape
    layers = blocks[0].shape[0] - 1
    heads = width // HD
    vmem = pl.BlockSpec(memory_space=pltpu.VMEM)
    smem = pl.BlockSpec(memory_space=pltpu.SMEM)
    if last:
        shapes = jax.ShapeDtypeStruct((layers, rows, width), jnp.bfloat16)
        out_specs = vmem
    else:
        shapes = (
            jax.ShapeDtypeStruct((layers, rows, width), jnp.float32),
            jax.ShapeDtypeStruct((heads, rows, HD), jnp.float32),
            jax.ShapeDtypeStruct((heads, rows, HD), jnp.float32),
        )
        out_specs = (vmem,) * 3
    state = () if state is None else tuple(state)
    count = len(blocks)
    work = 2 * rows * rows * width * count
    return pl.pallas_call(
        functools.partial(part_kernel, count, not state, last),
        out_shape=shapes,
        in_specs=[vmem, smem] + [vmem] * (count + len(state)),
        out_specs=out_specs,
        compiler_params=pltpu.CompilerParams(vmem_limit_bytes=32 * 1024 * 1024),
        cost_estimate=pl.CostEstimate(
            flops=work * (1 + layers),
            bytes_accessed=2 * rows * width * (1 + layers) * count,
            transcendentals=rows * rows * heads * count,
        ),
    )(queries, jnp.stack(live), *blocks, *state)


def body(queries, keys, values, tile_mask):
    here = lax.axis_index("ctx")
    c = here % CS
    x = here // CS % XS
    y = here // (CS * XS) % YS
    mask = tile_mask[0, :, 0, 0]

    def live(level, ahead):
        return jnp.where(ahead, mask[2 * level + 1], mask[2 * level + 2])

    own = jnp.concatenate([keys[None], values], axis=0)
    sign = lambda c: 1 if c else -1
    a1 = send(own, lambda z, y, x, c: (z + sign(c), y, x, c))
    yn = send(own, lambda z, y, x, c: (z, y + 1, x, c))
    x2n = send(own, lambda z, y, x, c: (z, y, x + 2, c))
    b1 = send(own, lambda z, y, x, c: (z - sign(c), y, x, c))
    cn = send(own, lambda z, y, x, c: (z, y, x, c + 1))
    a2 = send(a1, lambda z, y, x, c: (z + sign(c), y, x, c))
    b2 = send(b1, lambda z, y, x, c: (z - sign(c), y, x, c))
    yc = send(jnp.where((y == 0) == (c == 0), a1, b1), lambda z, y, x, c: (z, y + 1, x, c))
    a4 = send(a2, lambda z, y, x, c: (z + 2 * sign(c), y, x, c))
    b4 = send(b2, lambda z, y, x, c: (z - 2 * sign(c), y, x, c))
    above = jnp.where(y == 0, yn, yc)
    below = jnp.where(y == 0, yc, yn)
    x1u = send(jnp.where(x == XS - 1, below, own), lambda z, y, x, c: (z, y, x + 1, c))
    x1d = send(jnp.where(x == 0, above, own), lambda z, y, x, c: (z, y, x - 1, c))
    x2c = send(jnp.where(x < 2, above, below), lambda z, y, x, c: (z, y, x + 2, c))
    cc = send(jnp.where(c == 0, x1d, x1u), lambda z, y, x, c: (z, y, x, c + 1))

    up = c == 0
    state = attend(
        queries,
        [own, cn, yn, x2n, a1, b1, a2, b2, yc],
        [jnp.ones((), jnp.int32), live(0, up), live(3, y == 0), live(2, x < 2),
         live(4, up), live(4, ~up), live(5, up), live(5, ~up), live(3, y != 0)],
    )
    return attend(
        queries,
        [x1u, x1d, x2c, cc, a4, b4],
        [mask[4], mask[3], live(2, x >= 2), live(0, ~up), live(6, up), live(6, ~up)],
        state,
        last=True,
    )


def solution(mesh):
    in_specs = (P("ctx", "mp"), P("ctx", "mp"), P(None, "ctx", "mp"), P("ctx", None, None, None))
    out_specs = P(None, "ctx", "mp")
    return jax.shard_map(body, mesh=mesh, in_specs=in_specs, out_specs=out_specs, check_vma=False)
```

```python
import functools
import math

import jax
import jax.numpy as jnp
from jax import lax
from jax.experimental import pallas as pl
from jax.experimental.pallas import tpu as pltpu
from jax.sharding import PartitionSpec as P

HD = 128
DEAD = -1e30
MIB = 1024 * 1024
SPREAD = 1_000_000
GATE1, GATE2 = 20.0, 3.0
FIRST, LAST = 1, 1
ZS, YS, XS, CS = 16, 2, 4, 2


def place(z, y, x, c):
    return (((z % ZS) * YS + y % YS) * XS + x % XS) * CS + c % CS


def coordinates():
    here = lax.axis_index("ctx")
    return (here >> 3) & 1, (here >> 1) & 3, here & 1


ROWS = [
    [place(z, y, x, c) for x in range(XS)] for z in range(ZS) for y in range(YS) for c in range(CS)
]


def send(block, target):
    pairs = []
    for z in range(ZS):
        for y in range(YS):
            for x in range(XS):
                for c in range(CS):
                    goal = target(z, y, x, c)
                    if goal is not None:
                        pairs.append((place(z, y, x, c), place(*goal)))
    return lax.ppermute(block, "ctx", pairs)


def after(block, *others):
    return lax.optimization_barrier((block, *others))[0]


def attend_head(q_ref, blocks, biases, window, before=None):
    rows = q_ref.shape[0]
    layers = blocks[0].shape[0] - 1
    keys = jnp.concatenate([b[0, :, window] for b in blocks], axis=0)
    scores = lax.dot_general(
        q_ref[:, window], keys, (((1,), (1,)), ((), ())), preferred_element_type=jnp.float32
    ) * (math.log2(math.e) / math.sqrt(HD))
    parts = [
        scores[:, j * rows:(j + 1) * rows] + biases[j][...] for j in range(len(blocks))
    ]
    largest = jnp.max(functools.reduce(jnp.maximum, parts), axis=1, keepdims=True)
    if before is not None:
        largest = jnp.maximum(largest, before)
    probs = [jnp.exp2(s - largest) for s in parts]
    total = jnp.sum(functools.reduce(jnp.add, probs), axis=1, keepdims=True)
    weights = jnp.concatenate([p.astype(jnp.bfloat16) for p in probs], axis=1)
    values = jnp.concatenate(
        [jnp.concatenate([b[1 + layer, :, window] for layer in range(layers)], axis=1) for b in blocks],
        axis=0,
    )
    return largest, total, jnp.dot(weights, values, preferred_element_type=jnp.float32)


def first_kernel(stacked, rules, later, q_ref, mask_ref, *refs):
    blocks = []
    for ref, depth in zip(refs, stacked):
        blocks += [ref] if depth is None else [ref.at[j] for j in range(depth)]
    acc_ref, max_ref, sum_ref, later_ref, now_ref = refs[-5:]
    where = coordinates()
    row = (1, HD)
    for j, rule in enumerate(later):
        later_ref[j:j + 1] = jnp.where(rule(mask_ref, *where), jnp.zeros(row, jnp.float32), DEAD)
    for j, rule in enumerate(rules):
        now_ref[j:j + 1] = jnp.where(rule(mask_ref, *where), jnp.zeros(row, jnp.float32), DEAD)
    biases = [now_ref.at[j:j + 1] for j in range(len(rules))]
    for head in range(q_ref.shape[1] // HD):
        window = slice(head * HD, (head + 1) * HD)
        largest, total, acc = attend_head(q_ref, blocks, biases, window)
        max_ref[head] = jnp.broadcast_to(largest, max_ref.shape[1:])
        sum_ref[head] = jnp.broadcast_to(total, sum_ref.shape[1:])
        acc_ref[head] = acc


def last_kernel(count, q_ref, *refs):
    blocks = refs[:count]
    acc_ref, max_ref, sum_ref, bias_ref = refs[count:count + 4]
    out_ref = refs[-1]
    biases = [bias_ref.at[j:j + 1] for j in range(count)]
    for head in range(q_ref.shape[1] // HD):
        window = slice(head * HD, (head + 1) * HD)
        before = max_ref[head]
        largest, total, acc = attend_head(q_ref, blocks, biases, window, before)
        shrink = jnp.exp2(before - largest)
        inverse = 1.0 / (total + sum_ref[head] * shrink)
        for layer in range(out_ref.shape[0]):
            part = slice(layer * HD, (layer + 1) * HD)
            share = acc[:, part] + acc_ref[head, :, part] * shrink
            out_ref[layer, :, window] = (share * inverse).astype(out_ref.dtype)


def attend(queries, blocks, mask=None, later=None, state=(), tokens=()):
    rows, width = queries.shape
    heads = width // HD
    vmem = pl.BlockSpec(memory_space=pltpu.VMEM)
    operands = [queries]
    in_specs = [vmem]
    scratch = []
    if state:
        count = len(blocks)
        layers = blocks[0].shape[0] - 1
        kernel = functools.partial(last_kernel, count)
        shapes = jax.ShapeDtypeStruct((layers, rows, width), jnp.bfloat16)
        out_specs = vmem
    else:
        stacked = [block.shape[0] if rule is None else None for block, rule in blocks]
        rules = []
        for block, rule in blocks:
            rules += [beside(j) for j in range(block.shape[0])] if rule is None else [rule]
        blocks = [block for block, _ in blocks]
        count = len(rules)
        layers = blocks[0].shape[-3] - 1
        kernel = functools.partial(first_kernel, stacked, rules, later)
        operands.append(mask)
        in_specs.append(pl.BlockSpec(memory_space=pltpu.SMEM))
        shapes = (
            jax.ShapeDtypeStruct((heads, rows, layers * HD), jnp.float32),
            jax.ShapeDtypeStruct((heads, rows, HD), jnp.float32),
            jax.ShapeDtypeStruct((heads, rows, HD), jnp.float32),
            jax.ShapeDtypeStruct((8, HD), jnp.float32),
        )
        out_specs = (vmem,) * len(shapes)
        scratch = [pltpu.VMEM((16, HD), jnp.float32)]
    operands += [*blocks, *state, *tokens]
    in_specs += [vmem] * (len(blocks) + len(state) + len(tokens))
    return pl.pallas_call(
        kernel,
        out_shape=shapes,
        in_specs=in_specs,
        out_specs=out_specs,
        scratch_shapes=scratch,
        compiler_params=pltpu.CompilerParams(vmem_limit_bytes=8 * MIB),
        cost_estimate=pl.CostEstimate(
            flops=2 * rows * rows * width * count * (1 + layers) * (LAST if state else FIRST),
            bytes_accessed=2 * rows * width * (1 + layers) * count,
            transcendentals=rows * rows * heads * count,
        ),
    )(*operands)


def offset(level, ahead, there=None):
    def rule(mask_ref, y, x, c):
        up = ahead(y, x, c)
        alive = mask_ref[jnp.where(up, 2 * level + 1, 2 * level + 2)] != 0
        return alive if there is None else alive & there(y, x, c)

    return rule


def gate_kernel(*refs):
    refs[-1][...] = jnp.zeros_like(refs[-1])


def gate(weight, *arrays):
    vmem = pl.BlockSpec(memory_space=pltpu.VMEM)
    return pl.pallas_call(
        gate_kernel,
        out_shape=jax.ShapeDtypeStruct((8, 128), jnp.float32),
        in_specs=[pl.BlockSpec(memory_space=pl.ANY)] * len(arrays),
        out_specs=vmem,
        compiler_params=pltpu.CompilerParams(vmem_limit_bytes=1 * MIB),
        cost_estimate=pl.CostEstimate(flops=int(weight * 1e9), bytes_accessed=4096, transcendentals=0),
    )(*arrays)


def spread_kernel(own_ref, copies_ref, own_out_ref, sems):
    moves = [
        pltpu.make_async_copy(own_ref, goal, sems.at[j])
        for j, goal in enumerate([copies_ref.at[j] for j in range(XS)] + [own_out_ref])
    ]
    for move in moves:
        move.start()
    for move in moves:
        move.wait()


def spread(own):
    vmem = pl.BlockSpec(memory_space=pltpu.VMEM)
    anywhere = pl.BlockSpec(memory_space=pltpu.HBM)
    return pl.pallas_call(
        spread_kernel,
        out_shape=(
            jax.ShapeDtypeStruct((XS,) + own.shape, own.dtype),
            jax.ShapeDtypeStruct(own.shape, own.dtype),
        ),
        in_specs=[vmem],
        out_specs=(anywhere, anywhere),
        scratch_shapes=[pltpu.SemaphoreType.DMA((XS + 1,))],
        compiler_params=pltpu.CompilerParams(vmem_limit_bytes=3 * MIB),
        cost_estimate=pl.CostEstimate(flops=SPREAD, bytes_accessed=own.size, transcendentals=0),
    )(own)


def beside(j):
    def rule(mask_ref, y, x, c):
        ahead = j - x
        alive = mask_ref[jnp.where(ahead > 0, 1, 2) + 2 * jnp.abs(ahead)] != 0
        return (ahead == 0) | (alive & (jnp.abs(ahead) < 3))

    return rule


def body(queries, keys, values, tile_mask):
    y, x, c = coordinates()
    mask = tile_mask.reshape(-1)
    own = jnp.concatenate([keys[None], values], axis=0)
    sign = lambda y: 1 if y else -1

    a1 = send(own, lambda z, y, x, c: (z + sign(y), y, x, c))
    b1 = send(own, lambda z, y, x, c: (z - sign(y), y, x, c))
    copies, own = spread(own)
    row = lax.all_to_all(copies, "ctx", 0, 0, axis_index_groups=ROWS)
    cn = send(own, lambda z, y, x, c: (z, y, x, c + 1))
    yn = send(own, lambda z, y, x, c: (z, y + 1, x, c))
    token_a = gate(GATE1, a1)
    token_b = gate(GATE1, b1)
    a2 = send(after(a1, token_a), lambda z, y, x, c: (z + sign(y), y, x, c))
    b2 = send(after(b1, token_b), lambda z, y, x, c: (z - sign(y), y, x, c))
    edge = after(jnp.where((y == 0) == (x < 2), a1, own), cn, yn)
    x1w = send(edge, lambda z, y, x, c: (z, y + 1, 3 - x, c) if x in (0, 3) else None)
    x2c = send(edge, lambda z, y, x, c: (z, y + 1, x + 2, c))
    yc = send(after(a1, cn, yn), lambda z, y, x, c: (z, y + 1, x, c))
    a4 = send(a2, lambda z, y, x, c: (z + 2 * sign(y), y, x, c))
    b4 = send(b2, lambda z, y, x, c: (z - 2 * sign(y), y, x, c))
    state = attend(
        queries,
        [
            (row, None),
            (cn, offset(0, lambda y, x, c: c == 0)),
            (yn, offset(3, lambda y, x, c: y == 0)),
            (a1, offset(4, lambda y, x, c: y == 0)),
            (b1, offset(4, lambda y, x, c: y != 0)),
            (a2, offset(5, lambda y, x, c: y == 0)),
            (b2, offset(5, lambda y, x, c: y != 0)),
        ],
        mask=mask,
        tokens=[token_a, token_b],
        later=[
            offset(3, lambda y, x, c: y != 0),
            offset(2, lambda y, x, c: x >= 2),
            offset(1, lambda y, x, c: x == 3, lambda y, x, c: (x == 0) | (x == 3)),
            offset(0, lambda y, x, c: c != 0),
            offset(6, lambda y, x, c: y == 0),
            offset(6, lambda y, x, c: y != 0),
        ],
    )
    beside = lax.dynamic_index_in_dim(
        row, jnp.where(c == 0, jnp.minimum(x + 1, 3), jnp.maximum(x - 1, 0)), 0, keepdims=False
    )
    near = jnp.where(x == jnp.where(c == 0, 3, 0), x1w, beside)
    cc = send(after(near, state[3]), lambda z, y, x, c: (z, y, x, c + 1))
    token = gate(GATE2, a4, b4, x2c, yc, state[3])
    return attend(queries, [yc, x2c, x1w, cc, a4, b4], state=state, tokens=[token])


def solution(mesh):
    in_specs = (P("ctx", "mp"), P("ctx", "mp"), P(None, "ctx", "mp"), P("ctx", None, None, None))
    out_specs = P(None, "ctx", "mp")
    return jax.shard_map(body, mesh=mesh, in_specs=in_specs, out_specs=out_specs, check_vma=False)
```

```python
import functools
import math

import jax
import jax.numpy as jnp
from jax import lax
from jax.experimental import pallas as pl
from jax.experimental.pallas import tpu as pltpu
from jax.sharding import PartitionSpec as P

HD = 128
DEAD = -1e30
MIB = 1024 * 1024
GATE0, GATE1, GATE2 = 0.1, 20, 10.0
FIRST, LAST = 1, 1
ZS, YS, XS, CS = 16, 2, 4, 2


def place(z, y, x, c):
    return (((z % ZS) * YS + y % YS) * XS + x % XS) * CS + c % CS


def coordinates():
    here = lax.axis_index("ctx")
    return (here >> 3) & 1, (here >> 1) & 3, here & 1


def send(block, target):
    pairs = []
    for z in range(ZS):
        for y in range(YS):
            for x in range(XS):
                for c in range(CS):
                    goal = target(z, y, x, c)
                    if goal is not None:
                        pairs.append((place(z, y, x, c), place(*goal)))
    return lax.ppermute(block, "ctx", pairs)


def after(block, *others):
    return lax.optimization_barrier((block, *others))[0]


def attend_head(q_ref, blocks, biases, window, before=None):
    rows = q_ref.shape[0]
    layers = blocks[0].shape[0] - 1
    keys = jnp.concatenate([b[0, :, window] for b in blocks], axis=0)
    scores = lax.dot_general(
        q_ref[:, window], keys, (((1,), (1,)), ((), ())), preferred_element_type=jnp.float32
    ) * (math.log2(math.e) / math.sqrt(HD))
    parts = [
        scores[:, j * rows:(j + 1) * rows] + biases[j][...] for j in range(len(blocks))
    ]
    largest = jnp.max(functools.reduce(jnp.maximum, parts), axis=1, keepdims=True)
    if before is not None:
        largest = jnp.maximum(largest, before)
    probs = [jnp.exp2(s - largest) for s in parts]
    total = jnp.sum(functools.reduce(jnp.add, probs), axis=1, keepdims=True)
    weights = jnp.concatenate([p.astype(jnp.bfloat16) for p in probs], axis=1)
    values = jnp.concatenate(
        [jnp.concatenate([b[1 + layer, :, window] for layer in range(layers)], axis=1) for b in blocks],
        axis=0,
    )
    return largest, total, jnp.dot(weights, values, preferred_element_type=jnp.float32)


def first_kernel(rules, later, q_ref, mask_ref, *refs):
    blocks = refs[:len(rules)]
    acc_ref, max_ref, sum_ref, later_ref, now_ref = refs[-5:]
    where = coordinates()
    row = (1, HD)
    for j, rule in enumerate(later):
        later_ref[j:j + 1] = jnp.where(rule(mask_ref, *where), jnp.zeros(row, jnp.float32), DEAD)
    for j, rule in enumerate(rules):
        alive = True if rule is None else rule(mask_ref, *where)
        now_ref[j:j + 1] = jnp.where(alive, jnp.zeros(row, jnp.float32), DEAD)
    biases = [now_ref.at[j:j + 1] for j in range(len(rules))]
    for head in range(q_ref.shape[1] // HD):
        window = slice(head * HD, (head + 1) * HD)
        largest, total, acc = attend_head(q_ref, blocks, biases, window)
        max_ref[head] = jnp.broadcast_to(largest, max_ref.shape[1:])
        sum_ref[head] = jnp.broadcast_to(total, sum_ref.shape[1:])
        acc_ref[head] = acc


def last_kernel(count, q_ref, *refs):
    blocks = [*refs[:count - 1], refs[count - 1].at[0], refs[count - 1].at[1]]
    acc_ref, max_ref, sum_ref, bias_ref = refs[count:count + 4]
    out_ref = refs[-1]
    biases = [bias_ref.at[j:j + 1] for j in range(len(blocks))]
    for head in range(q_ref.shape[1] // HD):
        window = slice(head * HD, (head + 1) * HD)
        before = max_ref[head]
        largest, total, acc = attend_head(q_ref, blocks, biases, window, before)
        shrink = jnp.exp2(before - largest)
        inverse = 1.0 / (total + sum_ref[head] * shrink)
        for layer in range(out_ref.shape[0]):
            part = slice(layer * HD, (layer + 1) * HD)
            share = acc[:, part] + acc_ref[head, :, part] * shrink
            out_ref[layer, :, window] = (share * inverse).astype(out_ref.dtype)


def attend(queries, blocks, mask=None, later=None, state=(), tokens=()):
    rows, width = queries.shape
    heads = width // HD
    vmem = pl.BlockSpec(memory_space=pltpu.VMEM)
    operands = [queries]
    in_specs = [vmem]
    scratch = []
    if state:
        count = len(blocks)
        layers = blocks[0].shape[0] - 1
        kernel = functools.partial(last_kernel, count)
        shapes = jax.ShapeDtypeStruct((layers, rows, width), jnp.bfloat16)
        out_specs = vmem
    else:
        rules = [rule for _, rule in blocks]
        blocks = [block for block, _ in blocks]
        count = len(blocks)
        layers = blocks[0].shape[0] - 1
        kernel = functools.partial(first_kernel, rules, later)
        operands.append(mask)
        in_specs.append(pl.BlockSpec(memory_space=pltpu.SMEM))
        shapes = (
            jax.ShapeDtypeStruct((heads, rows, layers * HD), jnp.float32),
            jax.ShapeDtypeStruct((heads, rows, HD), jnp.float32),
            jax.ShapeDtypeStruct((heads, rows, HD), jnp.float32),
            jax.ShapeDtypeStruct((8, HD), jnp.float32),
        )
        out_specs = (vmem,) * len(shapes)
        scratch = [pltpu.VMEM((16, HD), jnp.float32)]
    operands += [*blocks, *state, *tokens]
    in_specs += [vmem] * (len(blocks) + len(state) + len(tokens))
    return pl.pallas_call(
        kernel,
        out_shape=shapes,
        in_specs=in_specs,
        out_specs=out_specs,
        scratch_shapes=scratch,
        compiler_params=pltpu.CompilerParams(vmem_limit_bytes=8 * MIB),
        cost_estimate=pl.CostEstimate(
            flops=2 * rows * rows * width * count * (1 + layers) * (LAST if state else FIRST),
            bytes_accessed=2 * rows * width * (1 + layers) * count,
            transcendentals=rows * rows * heads * count,
        ),
    )(*operands)


def offset(level, ahead):
    def rule(mask_ref, y, x, c):
        return mask_ref[jnp.where(ahead(y, x, c), 2 * level + 1, 2 * level + 2)] != 0

    return rule


def gate_kernel(*refs):
    refs[-1][...] = jnp.zeros_like(refs[-1])


def gate(weight, *arrays):
    vmem = pl.BlockSpec(memory_space=pltpu.VMEM)
    return pl.pallas_call(
        gate_kernel,
        out_shape=jax.ShapeDtypeStruct((8, 128), jnp.float32),
        in_specs=[pl.BlockSpec(memory_space=pl.ANY)] * len(arrays),
        out_specs=vmem,
        compiler_params=pltpu.CompilerParams(vmem_limit_bytes=1 * MIB),
        cost_estimate=pl.CostEstimate(flops=int(weight * 1e9), bytes_accessed=4096, transcendentals=0),
    )(*arrays)


def body(queries, keys, values, tile_mask):
    y, x, c = coordinates()
    mask = tile_mask.reshape(-1)
    own = jnp.concatenate([keys[None], values], axis=0)
    sign = lambda y: 1 if y else -1

    a1 = send(own, lambda z, y, x, c: (z + sign(y), y, x, c))
    b1 = send(own, lambda z, y, x, c: (z - sign(y), y, x, c))
    yn = send(own, lambda z, y, x, c: (z, y + 1, x, c))
    x1n = send(own, lambda z, y, x, c: (z, y, x ^ 1, c))
    x2n = send(after(own, b1), lambda z, y, x, c: (z, y, x + 2, c))
    token_a = gate(GATE1, a1)
    token_b = gate(GATE0, b1)
    a2 = send(after(a1, token_a), lambda z, y, x, c: (z + sign(y), y, x, c))
    b2 = send(after(b1, token_b), lambda z, y, x, c: (z - sign(y), y, x, c))
    edge = jnp.where((y == 0) == (x < 2), a1, own)
    inner = (x == 1) | (x == 2)
    x1w = send(
        after(jnp.where(inner, own, edge), yn),
        lambda z, y, x, c: (z, y if x in (1, 2) else y + 1, 3 - x, c),
    )
    x2c = send(edge, lambda z, y, x, c: (z, y + 1, x + 2, c))
    yc = send(after(a1, x1n), lambda z, y, x, c: (z, y + 1, x, c))
    a4 = send(a2, lambda z, y, x, c: (z + 2 * sign(y), y, x, c))
    b4 = send(b2, lambda z, y, x, c: (z - 2 * sign(y), y, x, c))
    state = attend(
        queries,
        [
            (own, None),
            (x1n, offset(1, lambda y, x, c: x & 1 == 0)),
            (x2n, offset(2, lambda y, x, c: x < 2)),
            (yn, offset(3, lambda y, x, c: y == 0)),
            (a1, offset(4, lambda y, x, c: y == 0)),
            (b1, offset(4, lambda y, x, c: y != 0)),
            (a2, offset(5, lambda y, x, c: y == 0)),
            (b2, offset(5, lambda y, x, c: y != 0)),
        ],
        mask=mask,
        tokens=[token_a, token_b],
        later=[
            offset(3, lambda y, x, c: y != 0),
            offset(2, lambda y, x, c: x >= 2),
            offset(1, lambda y, x, c: x & 1 == 1),
            offset(6, lambda y, x, c: y == 0),
            offset(6, lambda y, x, c: y != 0),
            offset(0, lambda y, x, c: c == 0),
            offset(0, lambda y, x, c: c != 0),
        ],
    )
    near = jnp.where(x & 1 == c, x1n, x1w)
    cc = send(after(jnp.stack([own, near]), state[3]), lambda z, y, x, c: (z, y, x, c + 1))
    token = gate(GATE2, a4, b4, x2c, yc, state[3])
    return attend(queries, [yc, x2c, x1w, a4, b4, cc], state=state, tokens=[token])


def solution(mesh):
    in_specs = (P("ctx", "mp"), P("ctx", "mp"), P(None, "ctx", "mp"), P("ctx", None, None, None))
    out_specs = P(None, "ctx", "mp")
    return jax.shard_map(body, mesh=mesh, in_specs=in_specs, out_specs=out_specs, check_vma=False)
```

```python
import functools
import math

import jax
import jax.numpy as jnp
from jax import lax
from jax.experimental import pallas as pl
from jax.experimental.pallas import tpu as pltpu
from jax.sharding import PartitionSpec as P

HD = 128
DEAD = -1e30
MIB = 1024 * 1024
GATE0, GATE1, GATE2 = 0.1, 20, 10.0
FIRST, LAST = 1, 1
ZS, YS, XS, CS = 16, 2, 4, 2


def place(z, y, x, c):
    return (((z % ZS) * YS + y % YS) * XS + x % XS) * CS + c % CS


def coordinates():
    here = lax.axis_index("ctx")
    return (here >> 3) & 1, (here >> 1) & 3, here & 1


def send(block, target):
    pairs = []
    for z in range(ZS):
        for y in range(YS):
            for x in range(XS):
                for c in range(CS):
                    goal = target(z, y, x, c)
                    if goal is not None:
                        pairs.append((place(z, y, x, c), place(*goal)))
    return lax.ppermute(block, "ctx", pairs)


def after(block, *others):
    return lax.optimization_barrier((block, *others))[0]


def weigh(q_ref, blocks, biases, window, before=None):
    rows = q_ref.shape[0]
    keys = jnp.concatenate([b[0, :, window] for b in blocks], axis=0)
    scores = lax.dot_general(
        q_ref[:, window], keys, (((1,), (1,)), ((), ())), preferred_element_type=jnp.float32
    ) * (math.log2(math.e) / math.sqrt(HD))
    parts = [
        scores[:, j * rows:(j + 1) * rows] + biases[j][...] for j in range(len(blocks))
    ]
    largest = jnp.max(functools.reduce(jnp.maximum, parts), axis=1, keepdims=True)
    if before is not None:
        largest = jnp.maximum(largest, before)
    probs = [jnp.exp2(s - largest) for s in parts]
    total = jnp.sum(functools.reduce(jnp.add, probs), axis=1, keepdims=True)
    return largest, total, jnp.concatenate([p.astype(jnp.bfloat16) for p in probs], axis=1)


def mix(weights, blocks, window):
    layers = blocks[0].shape[0] - 1
    values = jnp.concatenate(
        [jnp.concatenate([b[1 + layer, :, window] for layer in range(layers)], axis=1) for b in blocks],
        axis=0,
    )
    return jnp.dot(weights, values, preferred_element_type=jnp.float32)


def first_kernel(rules, later, q_ref, mask_ref, *refs):
    blocks = refs[:len(rules)]
    acc_ref, max_ref, sum_ref, later_ref, now_ref = refs[-5:]
    where = coordinates()
    row = (1, HD)
    for j, rule in enumerate(later):
        later_ref[j:j + 1] = jnp.where(rule(mask_ref, *where), jnp.zeros(row, jnp.float32), DEAD)
    for j, rule in enumerate(rules):
        alive = True if rule is None else rule(mask_ref, *where)
        now_ref[j:j + 1] = jnp.where(alive, jnp.zeros(row, jnp.float32), DEAD)
    biases = [now_ref.at[j:j + 1] for j in range(len(rules))]
    for head in range(q_ref.shape[1] // HD):
        window = slice(head * HD, (head + 1) * HD)
        largest, total, weights = weigh(q_ref, blocks, biases, window)
        max_ref[head] = jnp.broadcast_to(largest, max_ref.shape[1:])
        sum_ref[head] = jnp.broadcast_to(total, sum_ref.shape[1:])
        acc_ref[head] = mix(weights, blocks, window)


def last_kernel(count, q_ref, *refs):
    blocks = [*refs[:count - 1], refs[count - 1].at[0], refs[count - 1].at[1]]
    acc_ref, max_ref, sum_ref, bias_ref = refs[count:count + 4]
    out_ref = refs[-1]
    biases = [bias_ref.at[j:j + 1] for j in range(len(blocks))]
    heads = range(q_ref.shape[1] // HD)
    windows = [slice(head * HD, (head + 1) * HD) for head in heads]
    weighed = [weigh(q_ref, blocks, biases, windows[head], max_ref[head]) for head in heads]
    for head in heads:
        largest, total, weights = weighed[head]
        acc = mix(weights, blocks, windows[head])
        shrink = jnp.exp2(max_ref[head] - largest)
        inverse = 1.0 / (total + sum_ref[head] * shrink)
        for layer in range(out_ref.shape[0]):
            part = slice(layer * HD, (layer + 1) * HD)
            share = acc[:, part] + acc_ref[head, :, part] * shrink
            out_ref[layer, :, windows[head]] = (share * inverse).astype(out_ref.dtype)


def attend(queries, blocks, mask=None, later=None, state=(), tokens=()):
    rows, width = queries.shape
    heads = width // HD
    vmem = pl.BlockSpec(memory_space=pltpu.VMEM)
    operands = [queries]
    in_specs = [vmem]
    scratch = []
    if state:
        count = len(blocks)
        layers = blocks[0].shape[0] - 1
        kernel = functools.partial(last_kernel, count)
        shapes = jax.ShapeDtypeStruct((layers, rows, width), jnp.bfloat16)
        out_specs = vmem
    else:
        rules = [rule for _, rule in blocks]
        blocks = [block for block, _ in blocks]
        count = len(blocks)
        layers = blocks[0].shape[0] - 1
        kernel = functools.partial(first_kernel, rules, later)
        operands.append(mask)
        in_specs.append(pl.BlockSpec(memory_space=pltpu.SMEM))
        shapes = (
            jax.ShapeDtypeStruct((heads, rows, layers * HD), jnp.float32),
            jax.ShapeDtypeStruct((heads, rows, HD), jnp.float32),
            jax.ShapeDtypeStruct((heads, rows, HD), jnp.float32),
            jax.ShapeDtypeStruct((8, HD), jnp.float32),
        )
        out_specs = (vmem,) * len(shapes)
        scratch = [pltpu.VMEM((16, HD), jnp.float32)]
    operands += [*blocks, *state, *tokens]
    in_specs += [vmem] * (len(blocks) + len(state) + len(tokens))
    return pl.pallas_call(
        kernel,
        out_shape=shapes,
        in_specs=in_specs,
        out_specs=out_specs,
        scratch_shapes=scratch,
        compiler_params=pltpu.CompilerParams(vmem_limit_bytes=8 * MIB),
        cost_estimate=pl.CostEstimate(
            flops=2 * rows * rows * width * count * (1 + layers) * (LAST if state else FIRST),
            bytes_accessed=2 * rows * width * (1 + layers) * count,
            transcendentals=rows * rows * heads * count,
        ),
    )(*operands)


def offset(level, ahead):
    def rule(mask_ref, y, x, c):
        return mask_ref[jnp.where(ahead(y, x, c), 2 * level + 1, 2 * level + 2)] != 0

    return rule


def gate_kernel(*refs):
    refs[-1][...] = jnp.zeros_like(refs[-1])


def gate(weight, *arrays):
    vmem = pl.BlockSpec(memory_space=pltpu.VMEM)
    return pl.pallas_call(
        gate_kernel,
        out_shape=jax.ShapeDtypeStruct((8, 128), jnp.float32),
        in_specs=[pl.BlockSpec(memory_space=pl.ANY)] * len(arrays),
        out_specs=vmem,
        compiler_params=pltpu.CompilerParams(vmem_limit_bytes=1 * MIB),
        cost_estimate=pl.CostEstimate(flops=int(weight * 1e9), bytes_accessed=4096, transcendentals=0),
    )(*arrays)


def body(queries, keys, values, tile_mask):
    y, x, c = coordinates()
    mask = tile_mask.reshape(-1)
    own = jnp.concatenate([keys[None], values], axis=0)
    sign = lambda y: 1 if y else -1

    a1 = send(own, lambda z, y, x, c: (z + sign(y), y, x, c))
    b1 = send(own, lambda z, y, x, c: (z - sign(y), y, x, c))
    yn = send(own, lambda z, y, x, c: (z, y + 1, x, c))
    x1n = send(own, lambda z, y, x, c: (z, y, x ^ 1, c))
    x2n = send(after(own, b1), lambda z, y, x, c: (z, y, x + 2, c))
    token_a = gate(GATE1, a1)
    token_b = gate(GATE0, b1)
    a2 = send(after(a1, token_a), lambda z, y, x, c: (z + sign(y), y, x, c))
    b2 = send(after(b1, token_b), lambda z, y, x, c: (z - sign(y), y, x, c))
    edge = jnp.where((y == 0) == (x < 2), a1, own)
    inner = (x == 1) | (x == 2)
    x1w = send(
        after(jnp.where(inner, own, edge), yn),
        lambda z, y, x, c: (z, y if x in (1, 2) else y + 1, 3 - x, c),
    )
    x2c = send(edge, lambda z, y, x, c: (z, y + 1, x + 2, c))
    yc = send(after(a1, x1n), lambda z, y, x, c: (z, y + 1, x, c))
    a4 = send(a2, lambda z, y, x, c: (z + 2 * sign(y), y, x, c))
    b4 = send(b2, lambda z, y, x, c: (z - 2 * sign(y), y, x, c))
    state = attend(
        queries,
        [
            (own, None),
            (x1n, offset(1, lambda y, x, c: x & 1 == 0)),
            (x2n, offset(2, lambda y, x, c: x < 2)),
            (yn, offset(3, lambda y, x, c: y == 0)),
            (a1, offset(4, lambda y, x, c: y == 0)),
            (b1, offset(4, lambda y, x, c: y != 0)),
            (a2, offset(5, lambda y, x, c: y == 0)),
            (b2, offset(5, lambda y, x, c: y != 0)),
        ],
        mask=mask,
        tokens=[token_a, token_b],
        later=[
            offset(3, lambda y, x, c: y != 0),
            offset(2, lambda y, x, c: x >= 2),
            offset(1, lambda y, x, c: x & 1 == 1),
            offset(6, lambda y, x, c: y == 0),
            offset(6, lambda y, x, c: y != 0),
            offset(0, lambda y, x, c: c == 0),
            offset(0, lambda y, x, c: c != 0),
        ],
    )
    near = jnp.where(x & 1 == c, x1n, x1w)
    cc = send(after(jnp.stack([own, near]), state[3]), lambda z, y, x, c: (z, y, x, c + 1))
    token = gate(GATE2, a4, b4, x2c, yc, state[3])
    return attend(queries, [yc, x2c, x1w, a4, b4, cc], state=state, tokens=[token])


def solution(mesh):
    in_specs = (P("ctx", "mp"), P("ctx", "mp"), P(None, "ctx", "mp"), P("ctx", None, None, None))
    out_specs = P(None, "ctx", "mp")
    return jax.shard_map(body, mesh=mesh, in_specs=in_specs, out_specs=out_specs, check_vma=False)
```

```python
import functools
import math

import jax
import jax.numpy as jnp
from jax import lax
from jax.experimental import pallas as pl
from jax.experimental.pallas import tpu as pltpu
from jax.sharding import PartitionSpec as P

HD = 128
DEAD = -1e30
MIB = 1024 * 1024
GATE0, GATE1, GATE2 = 0.1, 20, 10.0
FIRST, LAST = 1, 1
ZS, YS, XS, CS = 16, 2, 4, 2


def place(z, y, x, c):
    return (((z % ZS) * YS + y % YS) * XS + x % XS) * CS + c % CS


def coordinates():
    here = lax.axis_index("ctx")
    return (here >> 3) & 1, (here >> 1) & 3, here & 1


def send(block, target):
    pairs = []
    for z in range(ZS):
        for y in range(YS):
            for x in range(XS):
                for c in range(CS):
                    goal = target(z, y, x, c)
                    if goal is not None:
                        pairs.append((place(z, y, x, c), place(*goal)))
    return lax.ppermute(block, "ctx", pairs)


def after(block, *others):
    return lax.optimization_barrier((block, *others))[0]


def score(q_ref, blocks, window):
    keys = jnp.concatenate([b[0, :, window] for b in blocks], axis=0)
    return lax.dot_general(
        q_ref[:, window], keys, (((1,), (1,)), ((), ())), preferred_element_type=jnp.float32
    ) * (math.log2(math.e) / math.sqrt(HD))


def weigh(scores, blocks, biases, before=None):
    rows = scores.shape[0]
    parts = [
        scores[:, j * rows:(j + 1) * rows] + biases[j][...] for j in range(len(blocks))
    ]
    largest = jnp.max(functools.reduce(jnp.maximum, parts), axis=1, keepdims=True)
    if before is not None:
        largest = jnp.maximum(largest, before)
    probs = [jnp.exp2(s - largest) for s in parts]
    total = jnp.sum(functools.reduce(jnp.add, probs), axis=1, keepdims=True)
    return largest, total, jnp.concatenate([p.astype(jnp.bfloat16) for p in probs], axis=1)


def mix(weights, blocks, window):
    layers = blocks[0].shape[0] - 1
    values = jnp.concatenate(
        [jnp.concatenate([b[1 + layer, :, window] for layer in range(layers)], axis=1) for b in blocks],
        axis=0,
    )
    return jnp.dot(weights, values, preferred_element_type=jnp.float32)


def first_kernel(rules, later, q_ref, mask_ref, *refs):
    blocks = refs[:len(rules)]
    acc_ref, max_ref, sum_ref, later_ref, now_ref = refs[-5:]
    where = coordinates()
    row = (1, HD)
    for j, rule in enumerate(later):
        later_ref[j:j + 1] = jnp.where(rule(mask_ref, *where), jnp.zeros(row, jnp.float32), DEAD)
    for j, rule in enumerate(rules):
        alive = True if rule is None else rule(mask_ref, *where)
        now_ref[j:j + 1] = jnp.where(alive, jnp.zeros(row, jnp.float32), DEAD)
    biases = [now_ref.at[j:j + 1] for j in range(len(rules))]
    for head in range(q_ref.shape[1] // HD):
        window = slice(head * HD, (head + 1) * HD)
        largest, total, weights = weigh(score(q_ref, blocks, window), blocks, biases)
        max_ref[head] = jnp.broadcast_to(largest, max_ref.shape[1:])
        sum_ref[head] = jnp.broadcast_to(total, sum_ref.shape[1:])
        acc_ref[head] = mix(weights, blocks, window)


def last_kernel(count, q_ref, *refs):
    blocks = [*refs[:count - 1], refs[count - 1].at[0], refs[count - 1].at[1]]
    acc_ref, max_ref, sum_ref, bias_ref = refs[count:count + 4]
    out_ref = refs[-1]
    biases = [bias_ref.at[j:j + 1] for j in range(len(blocks))]
    heads = range(q_ref.shape[1] // HD)
    windows = [slice(head * HD, (head + 1) * HD) for head in heads]
    scores = [score(q_ref, blocks, window) for window in windows]
    weighed = [weigh(scores[head], blocks, biases, max_ref[head]) for head in heads]
    for head in heads:
        largest, total, weights = weighed[head]
        acc = mix(weights, blocks, windows[head])
        shrink = jnp.exp2(max_ref[head] - largest)
        inverse = 1.0 / (total + sum_ref[head] * shrink)
        for layer in range(out_ref.shape[0]):
            part = slice(layer * HD, (layer + 1) * HD)
            share = acc[:, part] + acc_ref[head, :, part] * shrink
            out_ref[layer, :, windows[head]] = (share * inverse).astype(out_ref.dtype)


def attend(queries, blocks, mask=None, later=None, state=(), tokens=()):
    rows, width = queries.shape
    heads = width // HD
    vmem = pl.BlockSpec(memory_space=pltpu.VMEM)
    operands = [queries]
    in_specs = [vmem]
    scratch = []
    if state:
        count = len(blocks)
        layers = blocks[0].shape[0] - 1
        kernel = functools.partial(last_kernel, count)
        shapes = jax.ShapeDtypeStruct((layers, rows, width), jnp.bfloat16)
        out_specs = vmem
    else:
        rules = [rule for _, rule in blocks]
        blocks = [block for block, _ in blocks]
        count = len(blocks)
        layers = blocks[0].shape[0] - 1
        kernel = functools.partial(first_kernel, rules, later)
        operands.append(mask)
        in_specs.append(pl.BlockSpec(memory_space=pltpu.SMEM))
        shapes = (
            jax.ShapeDtypeStruct((heads, rows, layers * HD), jnp.float32),
            jax.ShapeDtypeStruct((heads, rows, HD), jnp.float32),
            jax.ShapeDtypeStruct((heads, rows, HD), jnp.float32),
            jax.ShapeDtypeStruct((8, HD), jnp.float32),
        )
        out_specs = (vmem,) * len(shapes)
        scratch = [pltpu.VMEM((16, HD), jnp.float32)]
    operands += [*blocks, *state, *tokens]
    in_specs += [vmem] * (len(blocks) + len(state) + len(tokens))
    return pl.pallas_call(
        kernel,
        out_shape=shapes,
        in_specs=in_specs,
        out_specs=out_specs,
        scratch_shapes=scratch,
        compiler_params=pltpu.CompilerParams(vmem_limit_bytes=8 * MIB),
        cost_estimate=pl.CostEstimate(
            flops=2 * rows * rows * width * count * (1 + layers) * (LAST if state else FIRST),
            bytes_accessed=2 * rows * width * (1 + layers) * count,
            transcendentals=rows * rows * heads * count,
        ),
    )(*operands)


def offset(level, ahead):
    def rule(mask_ref, y, x, c):
        return mask_ref[jnp.where(ahead(y, x, c), 2 * level + 1, 2 * level + 2)] != 0

    return rule


def gate_kernel(*refs):
    refs[-1][...] = jnp.zeros_like(refs[-1])


def gate(weight, *arrays):
    vmem = pl.BlockSpec(memory_space=pltpu.VMEM)
    return pl.pallas_call(
        gate_kernel,
        out_shape=jax.ShapeDtypeStruct((8, 128), jnp.float32),
        in_specs=[pl.BlockSpec(memory_space=pl.ANY)] * len(arrays),
        out_specs=vmem,
        compiler_params=pltpu.CompilerParams(vmem_limit_bytes=1 * MIB),
        cost_estimate=pl.CostEstimate(flops=int(weight * 1e9), bytes_accessed=4096, transcendentals=0),
    )(*arrays)


def body(queries, keys, values, tile_mask):
    y, x, c = coordinates()
    mask = tile_mask.reshape(-1)
    own = jnp.concatenate([keys[None], values], axis=0)
    sign = lambda y: 1 if y else -1

    a1 = send(own, lambda z, y, x, c: (z + sign(y), y, x, c))
    b1 = send(own, lambda z, y, x, c: (z - sign(y), y, x, c))
    yn = send(own, lambda z, y, x, c: (z, y + 1, x, c))
    x1n = send(own, lambda z, y, x, c: (z, y, x ^ 1, c))
    x2n = send(after(own, b1), lambda z, y, x, c: (z, y, x + 2, c))
    token_a = gate(GATE1, a1)
    token_b = gate(GATE0, b1)
    a2 = send(after(a1, token_a), lambda z, y, x, c: (z + sign(y), y, x, c))
    b2 = send(after(b1, token_b), lambda z, y, x, c: (z - sign(y), y, x, c))
    edge = jnp.where((y == 0) == (x < 2), a1, own)
    inner = (x == 1) | (x == 2)
    x1w = send(
        after(jnp.where(inner, own, edge), yn),
        lambda z, y, x, c: (z, y if x in (1, 2) else y + 1, 3 - x, c),
    )
    x2c = send(edge, lambda z, y, x, c: (z, y + 1, x + 2, c))
    yc = send(after(a1, x1n), lambda z, y, x, c: (z, y + 1, x, c))
    a4 = send(a2, lambda z, y, x, c: (z + 2 * sign(y), y, x, c))
    b4 = send(b2, lambda z, y, x, c: (z - 2 * sign(y), y, x, c))
    state = attend(
        queries,
        [
            (own, None),
            (x1n, offset(1, lambda y, x, c: x & 1 == 0)),
            (x2n, offset(2, lambda y, x, c: x < 2)),
            (yn, offset(3, lambda y, x, c: y == 0)),
            (a1, offset(4, lambda y, x, c: y == 0)),
            (b1, offset(4, lambda y, x, c: y != 0)),
            (a2, offset(5, lambda y, x, c: y == 0)),
            (b2, offset(5, lambda y, x, c: y != 0)),
        ],
        mask=mask,
        tokens=[token_a, token_b],
        later=[
            offset(3, lambda y, x, c: y != 0),
            offset(2, lambda y, x, c: x >= 2),
            offset(1, lambda y, x, c: x & 1 == 1),
            offset(6, lambda y, x, c: y == 0),
            offset(6, lambda y, x, c: y != 0),
            offset(0, lambda y, x, c: c == 0),
            offset(0, lambda y, x, c: c != 0),
        ],
    )
    near = jnp.where(x & 1 == c, x1n, x1w)
    cc = send(after(jnp.stack([own, near]), state[3]), lambda z, y, x, c: (z, y, x, c + 1))
    token = gate(GATE2, a4, b4, x2c, yc, state[3])
    return attend(queries, [yc, x2c, x1w, a4, b4, cc], state=state, tokens=[token])


def solution(mesh):
    in_specs = (P("ctx", "mp"), P("ctx", "mp"), P(None, "ctx", "mp"), P("ctx", None, None, None))
    out_specs = P(None, "ctx", "mp")
    return jax.shard_map(body, mesh=mesh, in_specs=in_specs, out_specs=out_specs, check_vma=False)
```
